256 devices in a mesh: tp: 16 (over z_lo, x), dp: 16 (over y, z_hi, core).
Axes of the slice: x: 4, y: 4, z: 8 (z_hi: 2, z_lo: 4; z = z_hi * 4 + z_lo), core: 2. Of those that a mesh axis runs over, the one named last changes fastest.
Arguments:
- img_tokens: bfloat16 [256, 64, 5120], P(None, 'dp', 'tp'), may hold values from -6 to 6
- key_weight: bfloat16 [5120, 5120], P('tp'), may hold values from -0.078125 to 0.078125
- value_map: bfloat16 [5120, 40], P('tp'), may hold values from -0.15625 to 0.15625
- queries: bfloat16 [256, 32, 5120], P('dp'), may hold values from -216 to 216
- cap_lengths: int32 [256], P('dp'), may hold values from 1 to 32
- candidates: int32 [64, 8], P('dp'), may hold values from 0 to 255, as said below
- counts: int32 [64], P('dp'), may hold values from 1 to 8
Outputs:
- pair_scores: float32 [64, 8], P('dp')
The draws below stay inside these ranges and needn't reach their ends.
Inputs may be any that keep to these rules, and one draw needn't show every extreme that they name: `candidates`: for every index g of dp and every index o of dp, exactly 2 of the 4 x 8 candidate slots (used or not) held at index g name a caption among o * 16 to (o + 1) * 16 - 1; the same caption may appear in several slots.
All inputs are finite; a program needn't handle non-finite values.
Results may differ from the reference program's by a relative error of at most 0.0003.
Values may be sent and summed in bfloat16 or wider, within the bound.
No kernel may reach another device: no remote copies, remote signals or barrier semaphores. Data moves between devices by JAX's collectives and lax.ppermute only.
A program may use at most 192 MiB of HBM per device.

```python
import jax
import jax.numpy as jnp
from jax import lax

D = 5120
H = 40
HD = 128
P_SIZE = 256
L = 32
TOP = 8
IMG_DP = 4
CAP_DP = 16
IMAGES = 64
CAPTIONS = 256
N_DP = 16


def draw_queries(key, part):
    first_key = jax.random.fold_in(key, 0)
    values = jnp.clip(jax.random.normal(first_key, (CAPTIONS, L, D), jnp.float32), -6.0, 6.0)
    return values.astype(jnp.bfloat16)


def draw_candidates(key, part):
    slot_total = IMG_DP * TOP
    owner_pool = jnp.tile(jnp.arange(N_DP, dtype=jnp.int32), slot_total // N_DP)

    def one_group(group_key):
        owners = jax.random.permutation(group_key, owner_pool)
        local_ids = jax.random.randint(jax.random.fold_in(group_key, 7), (slot_total,), 0, CAP_DP, dtype=jnp.int32)
        return (owners * CAP_DP + local_ids).reshape(IMG_DP, TOP)
    group_keys = jax.random.split(jax.random.fold_in(key, 11), N_DP)
    return jax.vmap(one_group)(group_keys).reshape(IMG_DP * N_DP, TOP).astype(jnp.int32)


def with_ends(values, own_key, least, top_value):
    dims = values.shape
    spot = [jax.random.randint(jax.random.fold_in(own_key, axis), (), 0, dims[axis]) for axis in range(len(dims))]
    values = values.at[tuple(spot)].set(least)
    longest = dims.index(max(dims))
    spot[longest] = (spot[longest] + 1) % dims[longest]
    return values.at[tuple(spot)].set(top_value)


def shard_levels(own_key, extent, shards, low, top_value):
    def one(position, blocks):
        heights = jax.random.uniform(jax.random.fold_in(jax.random.fold_in(own_key, 6), position), (blocks,), jnp.float32, low / len(shards), top_value / len(shards))
        return jnp.repeat(jnp.exp(heights), extent[position] // blocks).reshape((-1,) + (1,) * (len(extent) - position - 1))

    loudness = one(*shards[0])
    for cut in shards[1:]:
        loudness = loudness * one(*cut)
    return loudness


def scatter_about(rng, dims, scale, limit, cuts=(), kind=jnp.bfloat16):
    drawn = jax.random.normal(rng, dims, jnp.float32) * scale
    if len(cuts) > 0:
        drawn = shard_levels(rng, dims, cuts, -0.22, 0.18) * drawn
    return jnp.clip(drawn, min=-limit, max=limit).astype(kind)


def setup_inputs(seed: int = 0) -> dict:
    keys = jax.random.split(jax.random.key(seed), 8)
    return {
        "img_tokens": scatter_about(keys[0], (P_SIZE, IMAGES, D), 1.0, 6.0, ((1, 16), (2, 16))),
        "key_weight": scatter_about(keys[1], (D, D), D ** -0.5, 0.078125, ((0, 16),)),
        "value_map": scatter_about(keys[2], (D, H), (D // 4) ** -0.5, 0.15625, ((0, 16),)),
        "queries": draw_queries(jax.random.fold_in(keys[7], 71), 0),
        "cap_lengths": with_ends(jax.random.randint(keys[4], (CAPTIONS,), 1, L + 1), jax.random.fold_in(keys[4], 1), 1, L).astype(jnp.int32),
        "candidates": draw_candidates(jax.random.fold_in(keys[7], 71), 0),
        "counts": with_ends(jax.random.randint(keys[6], (IMAGES,), 1, TOP + 1), jax.random.fold_in(keys[6], 1), 1, TOP).astype(jnp.int32),
    }


def reference(img_tokens, key_weight, value_map, queries, cap_lengths, candidates, counts):
    total_rows = P_SIZE * IMAGES
    token_rows = img_tokens.reshape(total_rows, D)
    key_total = jnp.dot(token_rows, key_weight, preferred_element_type=jnp.float32)
    image_keys = key_total.reshape(P_SIZE, IMAGES, H, HD)
    patch_values = jnp.dot(token_rows, value_map, preferred_element_type=jnp.float32).reshape(P_SIZE, IMAGES, H)
    attn_scale = float(HD) ** -0.5

    def per_image(image_idx):
        cand_ids = candidates[image_idx]
        query_block = queries[cand_ids].reshape(TOP, L, H, HD).astype(jnp.float32)
        length_vals = cap_lengths[cand_ids]
        these_keys = lax.dynamic_index_in_dim(image_keys, image_idx, 1, keepdims=False)
        these_values = lax.dynamic_index_in_dim(patch_values, image_idx, 1, keepdims=False)
        logits = jnp.einsum('tlhd,phd->thlp', query_block, these_keys, precision=lax.Precision.HIGHEST) * attn_scale
        attention = jax.nn.softmax(logits, axis=-1)
        attended = jnp.einsum('thlp,ph->thl', attention, these_values, precision=lax.Precision.HIGHEST)
        token_live = (jnp.arange(L, dtype=jnp.int32)[None, :] < length_vals[:, None]).astype(jnp.float32)
        pair_score = jnp.sum(attended * token_live[:, None, :], axis=(1, 2)) / length_vals.astype(jnp.float32)
        slot_live = jnp.arange(TOP, dtype=jnp.int32) < counts[image_idx]
        return jnp.where(slot_live, pair_score, jnp.zeros_like(pair_score))

    return lax.map(per_image, jnp.arange(IMAGES, dtype=jnp.int32))
```

```python
import functools

import jax
import jax.numpy as jnp
from jax import lax
from jax.experimental import pallas as pl
from jax.experimental.pallas import tpu as pltpu
from jax.sharding import Mesh
from jax.sharding import PartitionSpec as P

H = 40
HD = 128
L = 32
TOP = 8
CAP_DP = 16
IMG = 4
GROUPS = 8
GH = H // GROUPS
GW = GH * HD
PATCH = 256
FEAT = 320
WIDE = 2 * FEAT
TP = ("zl", "x")
DP = ("y", "zh", "c")
YC = ("y", "c")


def pick_kernel(ids, col, q_ref, o_ref, sem):
    start = pl.multiple_of(col[0] * GW, 128)
    copies = []
    for r in range(2 * CAP_DP):
        copies.append(
            pltpu.make_async_copy(q_ref.at[ids[r], :, pl.ds(start, GW)], o_ref.at[r], sem.at[r])
        )
    for c in copies:
        c.start()
    for c in copies:
        c.wait()


def pick_queries(queries, ids, col):
    return pl.pallas_call(
        pick_kernel,
        out_shape=jax.ShapeDtypeStruct((2 * CAP_DP, L, GW), queries.dtype),
        in_specs=[
            pl.BlockSpec(memory_space=pltpu.SMEM),
            pl.BlockSpec(memory_space=pltpu.SMEM),
            pl.BlockSpec(memory_space=pl.ANY),
        ],
        out_specs=pl.BlockSpec(memory_space=pl.ANY),
        scratch_shapes=[pltpu.SemaphoreType.DMA((2 * CAP_DP,))],
        cost_estimate=pl.CostEstimate(flops=0, bytes_accessed=2 * 1310720, transcendentals=0),
        name="pick_queries",
    )(ids, col, queries)


def attend_kernel(order, slot, *refs):
    units = refs[:16]
    w_ref, v_ref, q_ref, o_ref = refs[16:20]
    xs, ws, vs, qs, acc, val, xsem, wsem, osem = refs[20:]
    xcopy = [pltpu.make_async_copy(units[u], xs.at[u], xsem.at[u]) for u in range(16)]
    wcopy = [pltpu.make_async_copy(w_ref.at[:, order[u]], ws.at[u], wsem.at[u]) for u in range(16)]
    vcopy = pltpu.make_async_copy(v_ref, vs, osem.at[0])
    qcopy = pltpu.make_async_copy(q_ref, qs, osem.at[1])
    vcopy.start()
    for u in range(16):
        wcopy[u].start()
        xcopy[u].start()
    qcopy.start()
    vcopy.wait()
    lane = lax.broadcasted_iota(jnp.int32, (PATCH, HD), 1)
    low = lane < HD // 2

    def rows_of(u):
        full = xs[u]
        rest = full[:, 512:640]
        zero = jnp.zeros_like(rest)
        first = jnp.concatenate([full[:, 0:256], jnp.where(low, rest, zero)], axis=1)
        second = jnp.concatenate([full[:, 256:512], jnp.where(low, zero, rest)], axis=1)
        return jnp.concatenate([first, second], axis=0)

    def weights_of(u):
        w = ws[u].astype(jnp.float32).reshape(FEAT, GW).astype(jnp.bfloat16)
        v = vs[order[u]]
        v = jnp.concatenate([v, v[:, 256:320]], axis=1)
        return jnp.concatenate([w, w[256:320]], axis=0), v

    for pair in range(8):
        a, b = 2 * pair, 2 * pair + 1
        for u in (a, b):
            wcopy[u].wait()
            xcopy[u].wait()
        x = jnp.concatenate([rows_of(a), rows_of(b)], axis=1)
        (wa, va), (wb, vb) = weights_of(a), weights_of(b)
        w = jnp.concatenate([wa, wb], axis=0)
        v = jnp.concatenate([va, vb], axis=1)
        keys = jnp.dot(x, w, preferred_element_type=jnp.float32)
        values = lax.dot_general(
            x, v, (((1,), (1,)), ((), ())), preferred_element_type=jnp.float32
        )
        if pair == 0:
            acc[...] = keys
            val[...] = values
        else:
            acc[...] += keys
            val[...] += values
    qcopy.wait()
    scale = float(HD) ** (-0.5)
    dims = (((1,), (1,)), ((), ()))
    for i in range(2):
        q = jnp.concatenate([qs[slot[TOP * i + k]] for k in range(TOP)], axis=0)
        total = jnp.zeros((1, TOP * L), jnp.float32)
        for h in range(GH):
            k = acc[PATCH * i : PATCH * (i + 1), HD * h : HD * (h + 1)]
            qh = q[:, HD * h : HD * (h + 1)]
            k1 = k.astype(jnp.bfloat16)
            r1 = k - k1.astype(jnp.float32)
            k2 = r1.astype(jnp.bfloat16)
            k3 = (r1 - k2.astype(jnp.float32)).astype(jnp.bfloat16)
            part = functools.partial(
                lax.dot_general, dimension_numbers=dims, preferred_element_type=jnp.float32
            )
            logits = (part(k3, qh) + part(k2, qh) + part(k1, qh)) * scale
            peak = jnp.max(logits, axis=0, keepdims=True)
            e = jnp.exp(logits - peak)
            norm = jnp.sum(e, axis=0, keepdims=True)
            v = val[PATCH * i : PATCH * (i + 1), h : h + 1]
            total = total + jnp.sum(e * v, axis=0, keepdims=True) / norm
        o_ref[i : i + 1, :] = total


def attend(order, slot, units, w, v, q):
    bf = jnp.bfloat16
    return pl.pallas_call(
        attend_kernel,
        out_shape=jax.ShapeDtypeStruct((2, TOP * L), jnp.float32),
        in_specs=[pl.BlockSpec(memory_space=pltpu.SMEM)] * 2
        + [pl.BlockSpec(memory_space=pl.ANY)] * 19,
        out_specs=pl.BlockSpec(memory_space=pltpu.VMEM),
        scratch_shapes=[
            pltpu.VMEM((16, PATCH, WIDE), bf),
            pltpu.VMEM((16, GROUPS, FEAT // 8, GW), bf),
            pltpu.VMEM((16, 8, FEAT), bf),
            pltpu.VMEM((2 * CAP_DP, L, GW), bf),
            pltpu.VMEM((2 * PATCH, GW), jnp.float32),
            pltpu.VMEM((2 * PATCH, 8), jnp.float32),
            pltpu.SemaphoreType.DMA((16,)),
            pltpu.SemaphoreType.DMA((16,)),
            pltpu.SemaphoreType.DMA((2,)),
        ],
        compiler_params=pltpu.CompilerParams(vmem_limit_bytes=44 * 2**20),
        cost_estimate=pl.CostEstimate(
            flops=2 * 512 * 5120 * 640, bytes_accessed=13 * 2**20, transcendentals=655360
        ),
        name="attend",
    )(order, slot, *units, w, v, q)


def shift(block, axis, by):
    return lax.ppermute(block, axis, [(i, (i + by) % 4) for i in range(4)])


def flip(block, mask):
    return lax.ppermute(block, "zl", [(i, i ^ mask) for i in range(4)])


def ring(unit):
    right = shift(unit, "x", 1)
    left = shift(unit, "x", -1)
    half = PATCH // 2
    top = shift(right[:half], "x", 1)
    bottom = shift(left[half:], "x", -1)
    return [unit, left, jnp.concatenate([top, bottom], axis=0), right]


def local(img_tokens, key_weight, value_map, queries, cap_lengths, candidates, counts):
    zl, x = lax.axis_index("zl"), lax.axis_index("x")
    half = zl // 2
    group = (zl % 2) * 4 + x
    me = lax.axis_index(DP)
    part = lax.axis_index(YC)

    slot_total = IMG * TOP
    cand_ids = candidates.reshape(slot_total)
    notice = jnp.broadcast_to(jnp.concatenate([cand_ids, cap_lengths])[None], (16, slot_total + CAP_DP))
    notices = lax.all_to_all(notice, DP, split_axis=0, concat_axis=0, tiled=True)

    tokens = img_tokens.reshape(PATCH, 2, 2, FEAT)
    packed = jnp.concatenate(
        [
            tokens[:, :, 0, :256],
            tokens[:, :, 1, :256],
            tokens[:, :, 0, 256:],
            tokens[:, :, 1, 256:],
        ],
        axis=-1,
    )
    mine = jnp.where(half == 0, packed[:, 0], packed[:, 1])
    theirs = jnp.where(half == 0, packed[:, 1], packed[:, 0])
    columns = [mine, flip(mine, 1), flip(theirs, 2), flip(theirs, 3)]
    units = [u for column in columns for u in ring(column)]
    order = jnp.stack([(zl ^ d) * 4 + (x + e) % 4 for d in range(4) for e in range(4)]).astype(jnp.int32)

    rows = FEAT // 8
    w_part = lax.dynamic_slice_in_dim(key_weight, part * rows, rows, axis=0)
    w_part = jnp.swapaxes(w_part.reshape(rows, GROUPS, GW), 0, 1)
    w_sent = jnp.concatenate([w_part, w_part], axis=0)
    w_mine = lax.all_to_all(w_sent, TP, split_axis=0, concat_axis=0, tiled=True)
    w_all = lax.all_gather(w_mine, YC)
    v_part = jnp.pad(value_map.T.reshape(GROUPS, GH, FEAT), ((0, 0), (0, 8 - GH), (0, 0)))
    v_all = lax.all_to_all(
        jnp.concatenate([v_part, v_part], axis=0), TP, split_axis=0, concat_axis=0, tiled=True
    )

    asked = notices[:, :slot_total]
    lengths = notices[:, slot_total:].reshape(16 * CAP_DP)
    match = (asked // CAP_DP) == me
    slots = jnp.arange(slot_total, dtype=jnp.int32)
    earlier = slots[:, None] > slots[None, :]
    rank = jnp.sum((match[:, None, :] & earlier[None]).astype(jnp.int32), axis=2)
    ids = jnp.sum(
        jnp.where(match[:, None, :] & (rank[:, None, :] == jnp.arange(2)[None, :, None]), asked[:, None, :] % CAP_DP, 0),
        axis=2,
    ).reshape(2 * CAP_DP)
    picked = pick_queries(queries, ids.astype(jnp.int32), group[None].astype(jnp.int32))
    replies = lax.all_to_all(
        picked.reshape(16, 2, L, GW), DP, split_axis=0, concat_axis=0, tiled=True
    ).reshape(2 * CAP_DP, L, GW)
    owners = cand_ids // CAP_DP
    own_rank = jnp.sum(((owners[:, None] == owners[None, :]) & earlier).astype(jnp.int32), axis=1)
    flat = (owners * 2 + own_rank).astype(jnp.int32)
    slot = jnp.where(half == 0, flat[:16], flat[16:])
    slot_lengths = jnp.sum(
        jnp.where(cand_ids[:, None] == jnp.arange(16 * CAP_DP, dtype=jnp.int32)[None, :], lengths[None, :], 0), axis=1
    )

    attended = attend(order, slot, units, w_all, v_all, replies)

    my_lengths = jnp.where(half == 0, slot_lengths[:16], slot_lengths[16:])
    live = jnp.arange(L, dtype=jnp.int32)[None, :] < my_lengths[:, None]
    sums = jnp.sum(jnp.where(live, attended.reshape(2 * TOP, L), 0.0), axis=1)
    everyone = lax.all_to_all(
        jnp.broadcast_to(sums[None], (16, 2 * TOP)), TP, split_axis=0, concat_axis=0, tiled=True
    )
    pair_sum = jnp.sum(everyone.reshape(2, GROUPS, 2 * TOP), axis=1).reshape(IMG, TOP)
    pair_score = pair_sum / slot_lengths.reshape(IMG, TOP).astype(jnp.float32)
    slot_live = jnp.arange(TOP, dtype=jnp.int32)[None, :] < counts[:, None]
    return jnp.where(slot_live, pair_score, jnp.zeros_like(pair_score))


def solution(mesh):
    fine = Mesh(mesh.devices.reshape(4, 4, 4, 2, 2), ("zl", "x", "y", "zh", "c"))
    in_specs = (
        P(None, DP, TP),
        P(TP, None),
        P(TP, None),
        P(DP, None, None),
        P(DP),
        P(DP, None),
        P(DP),
    )
    return jax.shard_map(local, mesh=fine, in_specs=in_specs, out_specs=P(DP, None), check_vma=False)
```

```python
import functools

import jax
import jax.numpy as jnp
from jax import lax
from jax.experimental import pallas as pl
from jax.experimental.pallas import tpu as pltpu
from jax.sharding import Mesh
from jax.sharding import PartitionSpec as P

H = 40
HD = 128
L = 32
TOP = 8
CAP_DP = 16
IMG = 4
GROUPS = 8
GH = H // GROUPS
GW = GH * HD
PATCH = 256
FEAT = 320
TP = ("zl", "x")
DP = ("y", "zh", "c")
YC = ("y", "c")


def pick_kernel(ids, col, q_ref, o_ref, sem):
    copies = []
    for r in range(2 * CAP_DP):
        start = pl.multiple_of(col[r] * GW, 128)
        copies.append(
            pltpu.make_async_copy(q_ref.at[ids[r], :, pl.ds(start, GW)], o_ref.at[r], sem.at[r])
        )
    for c in copies:
        c.start()
    for c in copies:
        c.wait()


def pick_queries(queries, ids, col):
    return pl.pallas_call(
        pick_kernel,
        out_shape=jax.ShapeDtypeStruct((2 * CAP_DP, L, GW), queries.dtype),
        in_specs=[
            pl.BlockSpec(memory_space=pltpu.SMEM),
            pl.BlockSpec(memory_space=pltpu.SMEM),
            pl.BlockSpec(memory_space=pltpu.HBM),
        ],
        out_specs=pl.BlockSpec(memory_space=pltpu.VMEM),
        scratch_shapes=[pltpu.SemaphoreType.DMA((2 * CAP_DP,))],
        compiler_params=pltpu.CompilerParams(vmem_limit_bytes=8 * 2**20),
        cost_estimate=pl.CostEstimate(flops=10**11, bytes_accessed=3 * 10**8, transcendentals=0),
        name="pick_queries",
    )(ids, col, queries)


def attend_kernel(order, slot, *refs):
    units = refs[:16]
    w_ref, v_ref, near_ref, far_ref, o_ref = refs[16:21]
    ws, q_ref, acc, val, wsem = refs[21:]
    wcopy = [pltpu.make_async_copy(w_ref.at[:, order[u]], ws.at[u], wsem.at[u]) for u in range(16)]
    for u in range(16):
        wcopy[u].start()

    for step in range(8):
        some = range(2 * step, 2 * step + 2)
        for u in some:
            wcopy[u].wait()
        w = jnp.concatenate(
            [ws[u].astype(jnp.float32).reshape(FEAT, GW).astype(jnp.bfloat16) for u in some], axis=0
        )
        v = jnp.concatenate([v_ref[order[u]] for u in some], axis=1)
        for i in range(2):
            x = jnp.concatenate([units[u][i] for u in some], axis=0)
            keys = lax.dot_general(
                x, w, (((0,), (0,)), ((), ())), preferred_element_type=jnp.float32
            )
            values = jnp.dot(v, x, preferred_element_type=jnp.float32)
            if step == 0:
                acc[i] = keys
                val[i] = values
            else:
                acc[i] += keys
                val[i] += values
    q_ref[0:CAP_DP] = near_ref[...]
    q_ref[CAP_DP:] = far_ref[...]
    scale = float(HD) ** (-0.5)
    part = functools.partial(
        lax.dot_general,
        dimension_numbers=(((1,), (1,)), ((), ())),
        preferred_element_type=jnp.float32,
    )
    for i in range(2):
        q = jnp.concatenate([q_ref[slot[TOP * i + k]] for k in range(TOP)], axis=0)
        v_all = val[i].T
        total = jnp.zeros((1, TOP * L), jnp.float32)
        for h in range(GH):
            k = acc[i, :, HD * h : HD * (h + 1)]
            qh = q[:, HD * h : HD * (h + 1)]
            k1 = k.astype(jnp.bfloat16)
            r1 = k - k1.astype(jnp.float32)
            k2 = r1.astype(jnp.bfloat16)
            k3 = (r1 - k2.astype(jnp.float32)).astype(jnp.bfloat16)
            logits = (part(k3, qh) + part(k2, qh) + part(k1, qh)) * scale
            peak = jnp.max(logits, axis=0, keepdims=True)
            e = jnp.exp(logits - peak)
            norm = jnp.sum(e, axis=0, keepdims=True)
            total = total + jnp.sum(e * v_all[:, h : h + 1], axis=0, keepdims=True) / norm
        o_ref[i : i + 1, :] = total


def attend(order, slot, units, w, v, near, far):
    vmem = pl.BlockSpec(memory_space=pltpu.VMEM)
    return pl.pallas_call(
        attend_kernel,
        out_shape=jax.ShapeDtypeStruct((2, TOP * L), jnp.float32),
        in_specs=[pl.BlockSpec(memory_space=pltpu.SMEM)] * 2
        + [vmem] * 16
        + [pl.BlockSpec(memory_space=pltpu.HBM)] + [vmem] * 3,
        out_specs=vmem,
        scratch_shapes=[
            pltpu.VMEM((16, GROUPS, FEAT // 8, GW), jnp.bfloat16),
            pltpu.VMEM((2 * CAP_DP, L, GW), jnp.bfloat16),
            pltpu.VMEM((2, PATCH, GW), jnp.float32),
            pltpu.VMEM((2, 8, PATCH), jnp.float32),
            pltpu.SemaphoreType.DMA((16,)),
        ],
        compiler_params=pltpu.CompilerParams(vmem_limit_bytes=52 * 2**20),
        cost_estimate=pl.CostEstimate(
            flops=2 * 512 * 5120 * 640, bytes_accessed=13 * 2**20, transcendentals=655360
        ),
        name="attend",
    )(order, slot, *units, w, v, near, far)


def mark_kernel(x_ref, o_ref):
    o_ref[...] = x_ref[...]


def mark(token, *held):
    token, *held = lax.optimization_barrier((token, *held))
    token = pl.pallas_call(
        mark_kernel,
        out_shape=jax.ShapeDtypeStruct(token.shape, token.dtype),
        in_specs=[pl.BlockSpec(memory_space=pltpu.VMEM)],
        out_specs=pl.BlockSpec(memory_space=pltpu.VMEM),
        compiler_params=pltpu.CompilerParams(vmem_limit_bytes=2**20),
        cost_estimate=pl.CostEstimate(flops=10**11, bytes_accessed=3 * 10**8, transcendentals=0),
        name="mark",
    )(token)
    return token, *held


def shift(block, axis, by):
    return lax.ppermute(block, axis, [(i, (i + by) % 4) for i in range(4)])


def flip(block, mask):
    return lax.ppermute(block, "zl", [(i, i ^ mask) for i in range(4)])


def ring(unit):
    return [unit, shift(unit, "x", -1), shift(unit, "x", 2), shift(unit, "x", 1)]


def local(img_tokens, key_weight, value_map, queries, cap_lengths, candidates, counts):
    zl, x, zh = lax.axis_index("zl"), lax.axis_index("x"), lax.axis_index("zh")
    half = zl // 2
    group = (zl % 2) * 4 + x
    me = lax.axis_index(DP)
    part = lax.axis_index(YC)

    rows = FEAT // 8
    w_part = lax.dynamic_slice_in_dim(key_weight, part * rows, rows, axis=0)
    w_part = jnp.swapaxes(w_part.reshape(rows, GROUPS, GW), 0, 1)
    v_part = jnp.pad(value_map.T.reshape(GROUPS, GH, FEAT), ((0, 0), (0, 8 - GH), (0, GW - FEAT)))
    w_part = jnp.concatenate([w_part, v_part], axis=1)
    w_sent = jnp.concatenate([w_part, w_part], axis=0)

    tokens = jnp.transpose(img_tokens, (1, 2, 0))
    mine = lax.dynamic_slice_in_dim(tokens, 2 * half, 2, axis=0)
    theirs = lax.dynamic_slice_in_dim(tokens, 2 - 2 * half, 2, axis=0)
    over = flip(theirs, 2)
    beside = flip(mine, 1)
    own = ring(mine)
    order = jnp.stack([(zl ^ d) * 4 + (x + e) % 4 for d in range(4) for e in range(4)]).astype(jnp.int32)

    slot_total = IMG * TOP
    cand_ids = candidates.reshape(slot_total)
    notice = jnp.broadcast_to(jnp.concatenate([cand_ids, cap_lengths])[None], (16, slot_total + CAP_DP))
    notice, mine, theirs = mark(notice, mine, theirs)
    notices = lax.all_to_all(notice, DP, split_axis=0, concat_axis=0, tiled=True)
    w_mine = lax.all_to_all(w_sent, TP, split_axis=0, concat_axis=0, tiled=True)
    w_mine, img_tokens = lax.optimization_barrier((w_mine, img_tokens))
    w_all = lax.all_gather(w_mine[:, :rows], YC)
    v_all = w_mine[:, rows:, :FEAT]

    notices, own, beside, over = lax.optimization_barrier((notices, own, beside, over))
    last = flip(over, 1)
    beside, over = ring(beside), ring(over)
    notices, last, *beside = mark(notices, last, *beside)

    asked = notices[:, :slot_total]
    lengths = notices[:, slot_total:].reshape(16 * CAP_DP)
    match = (asked // CAP_DP) == me
    slots = jnp.arange(slot_total, dtype=jnp.int32)
    earlier = slots[:, None] > slots[None, :]
    rank = jnp.sum((match[:, None, :] & earlier[None]).astype(jnp.int32), axis=2)
    ids = jnp.sum(
        jnp.where(match[:, None, :] & (rank[:, None, :] == jnp.arange(2)[None, :, None]), asked[:, None, :] % CAP_DP, 0),
        axis=2,
    ).reshape(2 * CAP_DP)
    same = (jnp.arange(2 * CAP_DP, dtype=jnp.int32) // 4) % 2 == zh
    columns = jnp.where(same, group, (1 - zl % 2) * 4 + x)
    picked = pick_queries(queries, ids.astype(jnp.int32), columns.astype(jnp.int32))
    picked = picked.reshape(4, 2, 2, 2, L, GW)
    near = lax.dynamic_index_in_dim(picked, zh, axis=1, keepdims=False)
    far = lax.dynamic_index_in_dim(picked, 1 - zh, axis=1, keepdims=False)
    far = lax.ppermute(far, ("zl", "zh"), [(2 * a + b, 2 * (3 - a) + 1 - b) for a in range(4) for b in range(2)])
    near = lax.all_to_all(near.reshape(8, 2, L, GW), YC, split_axis=0, concat_axis=0, tiled=True)
    last = ring(last)
    far, near, last, over = lax.optimization_barrier((far, near, last, over))
    far = lax.all_to_all(far.reshape(8, 2, L, GW), YC, split_axis=0, concat_axis=0, tiled=True)
    units = own + beside + over + last
    near = near.reshape(CAP_DP, L, GW)
    far = far.reshape(CAP_DP, L, GW)
    owners = cand_ids // CAP_DP
    own_rank = jnp.sum(((owners[:, None] == owners[None, :]) & earlier).astype(jnp.int32), axis=1)
    owner_zh = (owners // 2) % 2
    place = (owners // 4) * 2 + owners % 2
    flat = ((owner_zh ^ zh) * CAP_DP + place * 2 + own_rank).astype(jnp.int32)
    slot = jnp.where(half == 0, flat[:16], flat[16:])
    slot_lengths = jnp.sum(
        jnp.where(cand_ids[:, None] == jnp.arange(16 * CAP_DP, dtype=jnp.int32)[None, :], lengths[None, :], 0), axis=1
    )

    attended = attend(order, slot, units, w_all, v_all, near, far)

    my_lengths = jnp.where(half == 0, slot_lengths[:16], slot_lengths[16:])
    live = jnp.arange(L, dtype=jnp.int32)[None, :] < my_lengths[:, None]
    sums = jnp.sum(jnp.where(live, attended.reshape(2 * TOP, L), 0.0), axis=1)
    everyone = lax.all_to_all(
        jnp.broadcast_to(sums[None], (16, 2 * TOP)), TP, split_axis=0, concat_axis=0, tiled=True
    )
    pair_sum = jnp.sum(everyone.reshape(2, GROUPS, 2 * TOP), axis=1).reshape(IMG, TOP)
    pair_score = pair_sum / slot_lengths.reshape(IMG, TOP).astype(jnp.float32)
    slot_live = jnp.arange(TOP, dtype=jnp.int32)[None, :] < counts[:, None]
    return jnp.where(slot_live, pair_score, jnp.zeros_like(pair_score))


def solution(mesh):
    fine = Mesh(mesh.devices.reshape(4, 4, 4, 2, 2), ("zl", "x", "y", "zh", "c"))
    in_specs = (
        P(None, DP, TP),
        P(TP, None),
        P(TP, None),
        P(DP, None, None),
        P(DP),
        P(DP, None),
        P(DP),
    )
    return jax.shard_map(local, mesh=fine, in_specs=in_specs, out_specs=P(DP, None), check_vma=False)
```

```python
import functools

import jax
import jax.numpy as jnp
from jax import lax
from jax.experimental import pallas as pl
from jax.experimental.pallas import tpu as pltpu
from jax.sharding import Mesh
from jax.sharding import PartitionSpec as P

H = 40
HD = 128
L = 32
TOP = 8
CAP_DP = 16
IMG = 4
GROUPS = 8
GH = H // GROUPS
GW = GH * HD
PATCH = 256
FEAT = 320
ROWS = FEAT // 8
TP = ("zl", "x")
DP = ("y", "zh", "c")
YC = ("y", "c")


def pick_kernel(ids, col, q_ref, o_ref, sem):
    copies = []
    for r in range(2 * CAP_DP):
        start = pl.multiple_of(col[r] * GW, 128)
        copies.append(
            pltpu.make_async_copy(q_ref.at[ids[r], :, pl.ds(start, GW)], o_ref.at[r], sem.at[r])
        )
    for c in copies:
        c.start()
    for c in copies:
        c.wait()


def pick_queries(queries, ids, col):
    return pl.pallas_call(
        pick_kernel,
        out_shape=jax.ShapeDtypeStruct((2 * CAP_DP, L, GW), queries.dtype),
        in_specs=[
            pl.BlockSpec(memory_space=pltpu.SMEM),
            pl.BlockSpec(memory_space=pltpu.SMEM),
            pl.BlockSpec(memory_space=pltpu.HBM),
        ],
        out_specs=pl.BlockSpec(memory_space=pltpu.VMEM),
        scratch_shapes=[pltpu.SemaphoreType.DMA((2 * CAP_DP,))],
        compiler_params=pltpu.CompilerParams(vmem_limit_bytes=8 * 2**20),
        cost_estimate=pl.CostEstimate(flops=10**11, bytes_accessed=3 * 10**8, transcendentals=0),
        name="pick_queries",
    )(ids, col, queries)


def keys_kernel(order, *refs):
    units = refs[:16]
    w_ref, v_ref, acc, val = refs[16:20]
    ws, wsem = refs[20:]
    wcopy = [pltpu.make_async_copy(w_ref.at[:, order[u]], ws.at[u], wsem.at[u]) for u in range(16)]
    for u in range(16):
        wcopy[u].start()

    for step in range(8):
        some = range(2 * step, 2 * step + 2)
        for u in some:
            wcopy[u].wait()
        w = jnp.concatenate(
            [ws[u].astype(jnp.float32).reshape(FEAT, GW).astype(jnp.bfloat16) for u in some], axis=0
        )
        v = jnp.concatenate([v_ref[order[u]] for u in some], axis=1)
        for i in range(2):
            x = jnp.concatenate([units[u][i] for u in some], axis=0)
            keys = lax.dot_general(
                x, w, (((0,), (0,)), ((), ())), preferred_element_type=jnp.float32
            )
            values = jnp.dot(v, x, preferred_element_type=jnp.float32)
            if step == 0:
                acc[i] = keys
                val[i] = values
            else:
                acc[i] += keys
                val[i] += values


def project(order, units, w, v):
    vmem = pl.BlockSpec(memory_space=pltpu.VMEM)
    return pl.pallas_call(
        keys_kernel,
        out_shape=(
            jax.ShapeDtypeStruct((2, PATCH, GW), jnp.float32),
            jax.ShapeDtypeStruct((2, 8, PATCH), jnp.float32),
        ),
        in_specs=[pl.BlockSpec(memory_space=pltpu.SMEM)]
        + [vmem] * 16
        + [pl.BlockSpec(memory_space=pltpu.HBM), vmem],
        out_specs=(vmem, vmem),
        scratch_shapes=[
            pltpu.VMEM((16, 8, ROWS, GW), jnp.bfloat16),
            pltpu.SemaphoreType.DMA((16,)),
        ],
        compiler_params=pltpu.CompilerParams(vmem_limit_bytes=44 * 2**20),
        cost_estimate=pl.CostEstimate(
            flops=2 * 512 * 5120 * 640, bytes_accessed=13 * 2**20, transcendentals=0
        ),
        name="project",
    )(order, *units, w, v)


def attend_kernel(slot, acc, val, near_ref, far_ref, o_ref, q_ref):
    q_ref[0:CAP_DP] = near_ref[...]
    q_ref[CAP_DP:] = far_ref[...]
    scale = float(HD) ** (-0.5)
    part = functools.partial(
        lax.dot_general,
        dimension_numbers=(((1,), (1,)), ((), ())),
        preferred_element_type=jnp.float32,
    )
    for i in range(2):
        q = jnp.concatenate([q_ref[slot[TOP * i + k]] for k in range(TOP)], axis=0)
        v_all = val[i].T
        total = jnp.zeros((1, TOP * L), jnp.float32)
        for h in range(GH):
            k = acc[i, :, HD * h : HD * (h + 1)]
            qh = q[:, HD * h : HD * (h + 1)]
            k1 = k.astype(jnp.bfloat16)
            r1 = k - k1.astype(jnp.float32)
            k2 = r1.astype(jnp.bfloat16)
            k3 = (r1 - k2.astype(jnp.float32)).astype(jnp.bfloat16)
            logits = (part(k3, qh) + part(k2, qh) + part(k1, qh)) * scale
            peak = jnp.max(logits, axis=0, keepdims=True)
            e = jnp.exp(logits - peak)
            norm = jnp.sum(e, axis=0, keepdims=True)
            total = total + jnp.sum(e * v_all[:, h : h + 1], axis=0, keepdims=True) / norm
        o_ref[i : i + 1, :] = total


def attend(slot, keys, values, near, far):
    vmem = pl.BlockSpec(memory_space=pltpu.VMEM)
    return pl.pallas_call(
        attend_kernel,
        out_shape=jax.ShapeDtypeStruct((2, TOP * L), jnp.float32),
        in_specs=[pl.BlockSpec(memory_space=pltpu.SMEM)] + [vmem] * 4,
        out_specs=vmem,
        scratch_shapes=[pltpu.VMEM((2 * CAP_DP, L, GW), jnp.bfloat16)],
        compiler_params=pltpu.CompilerParams(vmem_limit_bytes=40 * 2**20),
        cost_estimate=pl.CostEstimate(
            flops=2 * 3 * 10 * 256 * 256 * 128, bytes_accessed=4 * 2**20, transcendentals=655360
        ),
        name="attend",
    )(slot, keys, values, near, far)


def mark_kernel(x_ref, o_ref):
    o_ref[...] = x_ref[...]


def mark(token, *held):
    if held:
        token, *held = lax.optimization_barrier((token, *held))
    token = pl.pallas_call(
        mark_kernel,
        out_shape=jax.ShapeDtypeStruct(token.shape, token.dtype),
        in_specs=[pl.BlockSpec(memory_space=pltpu.VMEM)],
        out_specs=pl.BlockSpec(memory_space=pltpu.VMEM),
        compiler_params=pltpu.CompilerParams(vmem_limit_bytes=2**20),
        cost_estimate=pl.CostEstimate(flops=10**11, bytes_accessed=3 * 10**8, transcendentals=0),
        name="mark",
    )(token)
    return token, *held


def shift(block, axis, by):
    return lax.ppermute(block, axis, [(i, (i + by) % 4) for i in range(4)])


def flip(block, mask):
    return lax.ppermute(block, "zl", [(i, i ^ mask) for i in range(4)])


def ring(unit):
    return [unit, shift(unit, "x", -1), shift(unit, "x", 2), shift(unit, "x", 1)]


def local(img_tokens, key_weight, value_map, queries, cap_lengths, candidates, counts):
    zl, x, zh = lax.axis_index("zl"), lax.axis_index("x"), lax.axis_index("zh")
    half = zl // 2
    group = (zl % 2) * 4 + x
    me = lax.axis_index(DP)
    part = lax.axis_index(YC)

    w_part = lax.dynamic_slice_in_dim(key_weight, part * ROWS, ROWS, axis=0)
    w_part = jnp.swapaxes(w_part.reshape(ROWS, GROUPS, GW), 0, 1)
    v_part = jnp.pad(value_map.T.reshape(GROUPS, GH, FEAT), ((0, 0), (0, 8 - GH), (0, GW - FEAT)))
    w_part = jnp.concatenate([w_part, v_part], axis=1)
    w_sent = jnp.concatenate([w_part, w_part], axis=0)

    tokens = jnp.transpose(img_tokens, (1, 2, 0))
    mine = lax.dynamic_slice_in_dim(tokens, 2 * half, 2, axis=0)
    theirs = lax.dynamic_slice_in_dim(tokens, 2 - 2 * half, 2, axis=0)
    over = flip(theirs, 2)
    beside = flip(mine, 1)
    own = ring(mine)
    order = jnp.stack([(zl ^ d) * 4 + (x + e) % 4 for d in range(4) for e in range(4)]).astype(jnp.int32)

    slot_total = IMG * TOP
    cand_ids = candidates.reshape(slot_total)
    notice = jnp.broadcast_to(jnp.concatenate([cand_ids, cap_lengths])[None], (16, slot_total + CAP_DP))
    notice, w_sent = mark(notice, w_sent)
    w_sent, notice = lax.optimization_barrier((w_sent, notice))
    w_mine = lax.all_to_all(w_sent, TP, split_axis=0, concat_axis=0, tiled=True)
    w_mine, v_all = w_mine[:, :ROWS], w_mine[:, ROWS:, :FEAT]
    w_mine, v_all, notice, own, beside, over = lax.optimization_barrier(
        (w_mine, v_all, notice, own, beside, over)
    )
    w_all = lax.all_gather(w_mine, YC)
    last = flip(over, 1)
    beside = ring(beside)
    (notice,) = mark(notice)
    notices = lax.all_to_all(notice, DP, split_axis=0, concat_axis=0, tiled=True)
    notices, beside, last = lax.optimization_barrier((notices, beside, last))
    over = ring(over)

    asked = notices[:, :slot_total]
    lengths = notices[:, slot_total:].reshape(16 * CAP_DP)
    match = (asked // CAP_DP) == me
    slots = jnp.arange(slot_total, dtype=jnp.int32)
    earlier = slots[:, None] > slots[None, :]
    rank = jnp.sum((match[:, None, :] & earlier[None]).astype(jnp.int32), axis=2)
    ids = jnp.sum(
        jnp.where(match[:, None, :] & (rank[:, None, :] == jnp.arange(2)[None, :, None]), asked[:, None, :] % CAP_DP, 0),
        axis=2,
    ).reshape(2 * CAP_DP)
    same = (jnp.arange(2 * CAP_DP, dtype=jnp.int32) // 4) % 2 == zh
    columns = jnp.where(same, group, (1 - zl % 2) * 4 + x)
    picked = pick_queries(queries, ids.astype(jnp.int32), columns.astype(jnp.int32))
    picked = picked.reshape(4, 2, 2, 2, L, GW)
    near = lax.dynamic_index_in_dim(picked, zh, axis=1, keepdims=False)
    far = lax.dynamic_index_in_dim(picked, 1 - zh, axis=1, keepdims=False)
    far = lax.ppermute(far, ("zl", "zh"), [(2 * a + b, 2 * (3 - a) + 1 - b) for a in range(4) for b in range(2)])
    near = lax.all_to_all(near.reshape(8, 2, L, GW), YC, split_axis=0, concat_axis=0, tiled=True)
    last = ring(last)
    far, near, last, over = lax.optimization_barrier((far, near, last, over))
    far = lax.all_to_all(far.reshape(8, 2, L, GW), YC, split_axis=0, concat_axis=0, tiled=True)
    units = own + beside + over + last
    near = near.reshape(CAP_DP, L, GW)
    far = far.reshape(CAP_DP, L, GW)
    owners = cand_ids // CAP_DP
    own_rank = jnp.sum(((owners[:, None] == owners[None, :]) & earlier).astype(jnp.int32), axis=1)
    owner_zh = (owners // 2) % 2
    place = (owners // 4) * 2 + owners % 2
    flat = ((owner_zh ^ zh) * CAP_DP + place * 2 + own_rank).astype(jnp.int32)
    slot = jnp.where(half == 0, flat[:16], flat[16:])
    slot_lengths = jnp.sum(
        jnp.where(cand_ids[:, None] == jnp.arange(16 * CAP_DP, dtype=jnp.int32)[None, :], lengths[None, :], 0), axis=1
    )

    keys, values = project(order, units, w_all, v_all)
    attended = attend(slot, keys, values, near, far)

    my_lengths = jnp.where(half == 0, slot_lengths[:16], slot_lengths[16:])
    live = jnp.arange(L, dtype=jnp.int32)[None, :] < my_lengths[:, None]
    sums = jnp.sum(jnp.where(live, attended.reshape(2 * TOP, L), 0.0), axis=1)
    everyone = lax.all_to_all(
        jnp.broadcast_to(sums[None], (16, 2 * TOP)), TP, split_axis=0, concat_axis=0, tiled=True
    )
    pair_sum = jnp.sum(everyone.reshape(2, GROUPS, 2 * TOP), axis=1).reshape(IMG, TOP)
    pair_score = pair_sum / slot_lengths.reshape(IMG, TOP).astype(jnp.float32)
    slot_live = jnp.arange(TOP, dtype=jnp.int32)[None, :] < counts[:, None]
    return jnp.where(slot_live, pair_score, jnp.zeros_like(pair_score))


def solution(mesh):
    fine = Mesh(mesh.devices.reshape(4, 4, 4, 2, 2), ("zl", "x", "y", "zh", "c"))
    in_specs = (
        P(None, DP, TP),
        P(TP, None),
        P(TP, None),
        P(DP, None, None),
        P(DP),
        P(DP, None),
        P(DP),
    )
    return jax.shard_map(local, mesh=fine, in_specs=in_specs, out_specs=P(DP, None), check_vma=False)
```

```python
import functools

import jax
import jax.numpy as jnp
from jax import lax
from jax.experimental import pallas as pl
from jax.experimental.pallas import tpu as pltpu
from jax.sharding import Mesh
from jax.sharding import PartitionSpec as P

H = 40
HD = 128
L = 32
TOP = 8
CAP_DP = 16
IMG = 4
GROUPS = 8
GH = H // GROUPS
GW = GH * HD
PATCH = 256
FEAT = 320
ROWS = FEAT // 8
TP = ("zl", "x")
DP = ("y", "zh", "c")
YC = ("y", "c")


def pick_kernel(ids, col, q_ref, o_ref, sem):
    copies = []
    for r in range(2 * CAP_DP):
        start = pl.multiple_of(col[r] * GW, 128)
        copies.append(
            pltpu.make_async_copy(q_ref.at[ids[r], :, pl.ds(start, GW)], o_ref.at[r], sem.at[r])
        )
    for c in copies:
        c.start()
    for c in copies:
        c.wait()


def pick_queries(queries, ids, col):
    return pl.pallas_call(
        pick_kernel,
        out_shape=jax.ShapeDtypeStruct((2 * CAP_DP, L, GW), queries.dtype),
        in_specs=[
            pl.BlockSpec(memory_space=pltpu.SMEM),
            pl.BlockSpec(memory_space=pltpu.SMEM),
            pl.BlockSpec(memory_space=pltpu.HBM),
        ],
        out_specs=pl.BlockSpec(memory_space=pltpu.VMEM),
        scratch_shapes=[pltpu.SemaphoreType.DMA((2 * CAP_DP,))],
        compiler_params=pltpu.CompilerParams(vmem_limit_bytes=52 * 2**20),
        cost_estimate=pl.CostEstimate(flops=10**11, bytes_accessed=3 * 10**8, transcendentals=0),
        name="pick_queries",
    )(ids, col, queries)


def keys_kernel(order, *refs):
    units = refs[:16]
    w_ref, v_ref, acc, val = refs[16:20]
    ws, wsem = refs[20:]
    wcopy = [pltpu.make_async_copy(w_ref.at[:, order[u]], ws.at[u], wsem.at[u]) for u in range(16)]
    for u in range(16):
        wcopy[u].start()

    for step in range(8):
        some = range(2 * step, 2 * step + 2)
        for u in some:
            wcopy[u].wait()
        w = jnp.concatenate(
            [ws[u].astype(jnp.float32).reshape(FEAT, GW).astype(jnp.bfloat16) for u in some], axis=0
        )
        v = jnp.concatenate([v_ref[order[u]] for u in some], axis=1)
        for i in range(2):
            x = jnp.concatenate([units[u][i] for u in some], axis=0)
            keys = lax.dot_general(
                x, w, (((0,), (0,)), ((), ())), preferred_element_type=jnp.float32
            )
            values = jnp.dot(v, x, preferred_element_type=jnp.float32)
            if step == 0:
                acc[i] = keys
                val[i] = values
            else:
                acc[i] += keys
                val[i] += values


def project(order, units, w, v):
    vmem = pl.BlockSpec(memory_space=pltpu.VMEM)
    return pl.pallas_call(
        keys_kernel,
        out_shape=(
            jax.ShapeDtypeStruct((2, PATCH, GW), jnp.float32),
            jax.ShapeDtypeStruct((2, 8, PATCH), jnp.float32),
        ),
        in_specs=[pl.BlockSpec(memory_space=pltpu.SMEM)]
        + [vmem] * 16
        + [pl.BlockSpec(memory_space=pltpu.HBM), vmem],
        out_specs=(vmem, vmem),
        scratch_shapes=[
            pltpu.VMEM((16, 8, ROWS, GW), jnp.bfloat16),
            pltpu.SemaphoreType.DMA((16,)),
        ],
        compiler_params=pltpu.CompilerParams(vmem_limit_bytes=44 * 2**20),
        cost_estimate=pl.CostEstimate(
            flops=2 * 512 * 5120 * 640, bytes_accessed=13 * 2**20, transcendentals=0
        ),
        name="project",
    )(order, *units, w, v)


def attend_kernel(slot, acc, val, near_ref, far_ref, o_ref, q_ref, sem):
    copies = [
        pltpu.make_async_copy(near_ref, q_ref.at[pl.ds(0, CAP_DP)], sem.at[0]),
        pltpu.make_async_copy(far_ref, q_ref.at[pl.ds(CAP_DP, CAP_DP)], sem.at[1]),
    ]
    for c in copies:
        c.start()
    for c in copies:
        c.wait()
    scale = float(HD) ** (-0.5)
    part = functools.partial(
        lax.dot_general,
        dimension_numbers=(((1,), (1,)), ((), ())),
        preferred_element_type=jnp.float32,
    )
    for i in range(2):
        q = jnp.concatenate([q_ref[slot[TOP * i + k]] for k in range(TOP)], axis=0)
        v_all = val[i].T
        total = jnp.zeros((1, TOP * L), jnp.float32)
        for h in range(GH):
            k = acc[i, :, HD * h : HD * (h + 1)]
            qh = q[:, HD * h : HD * (h + 1)]
            k1 = k.astype(jnp.bfloat16)
            r1 = k - k1.astype(jnp.float32)
            k2 = r1.astype(jnp.bfloat16)
            k3 = (r1 - k2.astype(jnp.float32)).astype(jnp.bfloat16)
            logits = (part(k3, qh) + part(k2, qh) + part(k1, qh)) * scale
            peak = jnp.max(logits, axis=0, keepdims=True)
            e = jnp.exp(logits - peak)
            norm = jnp.sum(e, axis=0, keepdims=True)
            total = total + jnp.sum(e * v_all[:, h : h + 1], axis=0, keepdims=True) / norm
        o_ref[i : i + 1, :] = total


def attend(slot, keys, values, near, far):
    vmem = pl.BlockSpec(memory_space=pltpu.VMEM)
    return pl.pallas_call(
        attend_kernel,
        out_shape=jax.ShapeDtypeStruct((2, TOP * L), jnp.float32),
        in_specs=[pl.BlockSpec(memory_space=pltpu.SMEM), vmem, vmem]
        + [pl.BlockSpec(memory_space=pltpu.HBM)] * 2,
        out_specs=vmem,
        scratch_shapes=[
            pltpu.VMEM((2 * CAP_DP, L, GW), jnp.bfloat16),
            pltpu.SemaphoreType.DMA((2,)),
        ],
        compiler_params=pltpu.CompilerParams(vmem_limit_bytes=40 * 2**20),
        cost_estimate=pl.CostEstimate(
            flops=2 * 3 * 10 * 256 * 256 * 128, bytes_accessed=4 * 2**20, transcendentals=655360
        ),
        name="attend",
    )(slot, keys, values, near, far)


def mark_kernel(x_ref, o_ref):
    o_ref[...] = x_ref[...]


def mark(token, *held):
    if held:
        token, *held = lax.optimization_barrier((token, *held))
    token = pl.pallas_call(
        mark_kernel,
        out_shape=jax.ShapeDtypeStruct(token.shape, token.dtype),
        in_specs=[pl.BlockSpec(memory_space=pltpu.VMEM)],
        out_specs=pl.BlockSpec(memory_space=pltpu.VMEM),
        compiler_params=pltpu.CompilerParams(vmem_limit_bytes=2**20),
        cost_estimate=pl.CostEstimate(flops=10**11, bytes_accessed=3 * 10**8, transcendentals=0),
        name="mark",
    )(token)
    return token, *held


def shift(block, axis, by):
    return lax.ppermute(block, axis, [(i, (i + by) % 4) for i in range(4)])


def flip(block, mask):
    return lax.ppermute(block, "zl", [(i, i ^ mask) for i in range(4)])


def ring(unit):
    return [unit, shift(unit, "x", -1), shift(unit, "x", 2), shift(unit, "x", 1)]


def local(img_tokens, key_weight, value_map, queries, cap_lengths, candidates, counts):
    zl, x, zh = lax.axis_index("zl"), lax.axis_index("x"), lax.axis_index("zh")
    half = zl // 2
    group = (zl % 2) * 4 + x
    me = lax.axis_index(DP)
    part = lax.axis_index(YC)

    w_part = lax.dynamic_slice_in_dim(key_weight, part * ROWS, ROWS, axis=0)
    w_part = jnp.swapaxes(w_part.reshape(ROWS, GROUPS, GW), 0, 1)
    v_part = jnp.pad(value_map.T.reshape(GROUPS, GH, FEAT), ((0, 0), (0, 8 - GH), (0, GW - FEAT)))
    w_part = jnp.concatenate([w_part, v_part], axis=1)
    w_sent = jnp.concatenate([w_part, w_part], axis=0)

    tokens = jnp.transpose(img_tokens, (1, 2, 0))
    mine = lax.dynamic_slice_in_dim(tokens, 2 * half, 2, axis=0)
    theirs = lax.dynamic_slice_in_dim(tokens, 2 - 2 * half, 2, axis=0)
    over = flip(theirs, 2)
    beside = flip(mine, 1)
    own = ring(mine)
    order = jnp.stack([(zl ^ d) * 4 + (x + e) % 4 for d in range(4) for e in range(4)]).astype(jnp.int32)

    slot_total = IMG * TOP
    cand_ids = candidates.reshape(slot_total)
    notice = jnp.broadcast_to(jnp.concatenate([cand_ids, cap_lengths])[None], (16, slot_total + CAP_DP))
    notice, w_sent = mark(notice, w_sent)
    w_sent, notice = lax.optimization_barrier((w_sent, notice))
    w_mine = lax.all_to_all(w_sent, TP, split_axis=0, concat_axis=0, tiled=True)
    w_mine, v_all = w_mine[:, :ROWS], w_mine[:, ROWS:, :FEAT]
    w_mine, v_all, notice, own, beside, over = lax.optimization_barrier(
        (w_mine, v_all, notice, own, beside, over)
    )
    w_all = lax.all_gather(w_mine, YC)
    last = flip(over, 1)
    beside = ring(beside)
    (notice,) = mark(notice)
    notices = lax.all_to_all(notice, DP, split_axis=0, concat_axis=0, tiled=True)
    notices, beside, last = lax.optimization_barrier((notices, beside, last))
    over = ring(over)

    asked = notices[:, :slot_total]
    lengths = notices[:, slot_total:].reshape(16 * CAP_DP)
    match = (asked // CAP_DP) == me
    slots = jnp.arange(slot_total, dtype=jnp.int32)
    earlier = slots[:, None] > slots[None, :]
    rank = jnp.sum((match[:, None, :] & earlier[None]).astype(jnp.int32), axis=2)
    ids = jnp.sum(
        jnp.where(match[:, None, :] & (rank[:, None, :] == jnp.arange(2)[None, :, None]), asked[:, None, :] % CAP_DP, 0),
        axis=2,
    ).reshape(2 * CAP_DP)
    same = (jnp.arange(2 * CAP_DP, dtype=jnp.int32) // 4) % 2 == zh
    columns = jnp.where(same, group, (1 - zl % 2) * 4 + x)
    picked = pick_queries(queries, ids.astype(jnp.int32), columns.astype(jnp.int32))
    picked = picked.reshape(4, 2, 2, 2, L, GW)
    near = lax.dynamic_index_in_dim(picked, zh, axis=1, keepdims=False)
    far = lax.dynamic_index_in_dim(picked, 1 - zh, axis=1, keepdims=False)
    far = lax.ppermute(far, ("zl", "zh"), [(2 * a + b, 2 * (3 - a) + 1 - b) for a in range(4) for b in range(2)])
    near = lax.all_to_all(near.reshape(8, 2, L, GW), YC, split_axis=0, concat_axis=0, tiled=True)
    last = ring(last)
    far, near, last, over = lax.optimization_barrier((far, near, last, over))
    far = lax.all_to_all(far.reshape(8, 2, L, GW), YC, split_axis=0, concat_axis=0, tiled=True)
    units = own + beside + over + last
    near = near.reshape(CAP_DP, L, GW)
    far = far.reshape(CAP_DP, L, GW)
    owners = cand_ids // CAP_DP
    own_rank = jnp.sum(((owners[:, None] == owners[None, :]) & earlier).astype(jnp.int32), axis=1)
    owner_zh = (owners // 2) % 2
    place = (owners // 4) * 2 + owners % 2
    flat = ((owner_zh ^ zh) * CAP_DP + place * 2 + own_rank).astype(jnp.int32)
    slot = jnp.where(half == 0, flat[:16], flat[16:])
    slot_lengths = jnp.sum(
        jnp.where(cand_ids[:, None] == jnp.arange(16 * CAP_DP, dtype=jnp.int32)[None, :], lengths[None, :], 0), axis=1
    )

    keys, values = project(order, units, w_all, v_all)
    attended = attend(slot, keys, values, near, far)

    my_lengths = jnp.where(half == 0, slot_lengths[:16], slot_lengths[16:])
    live = jnp.arange(L, dtype=jnp.int32)[None, :] < my_lengths[:, None]
    sums = jnp.sum(jnp.where(live, attended.reshape(2 * TOP, L), 0.0), axis=1)
    everyone = lax.all_to_all(
        jnp.broadcast_to(sums[None], (16, 2 * TOP)), TP, split_axis=0, concat_axis=0, tiled=True
    )
    pair_sum = jnp.sum(everyone.reshape(2, GROUPS, 2 * TOP), axis=1).reshape(IMG, TOP)
    pair_score = pair_sum / slot_lengths.reshape(IMG, TOP).astype(jnp.float32)
    slot_live = jnp.arange(TOP, dtype=jnp.int32)[None, :] < counts[:, None]
    return jnp.where(slot_live, pair_score, jnp.zeros_like(pair_score))


def solution(mesh):
    fine = Mesh(mesh.devices.reshape(4, 4, 4, 2, 2), ("zl", "x", "y", "zh", "c"))
    in_specs = (
        P(None, DP, TP),
        P(TP, None),
        P(TP, None),
        P(DP, None, None),
        P(DP),
        P(DP, None),
        P(DP),
    )
    return jax.shard_map(local, mesh=fine, in_specs=in_specs, out_specs=P(DP, None), check_vma=False)
```
